32 devices in a mesh: gx: 4 (over z), gy: 2 (over y), gz: 4 (over x, core).
Axes of the slice: x: 2, y: 2, z: 4, core: 2. Of those that a mesh axis runs over, the one named last changes fastest.
Arguments:
- tokens: bfloat16 [128, 4096], P(('gy', 'gz'), 'gx'), may hold values from -6 to 6
- expert_ids: int32 [128, 2], P(('gy', 'gz')), may hold values from 0 to 7, all different within a row; in each aligned block of 16 rows (0 to 15, 16 to 31, ...) at most 8 rows name the same one
- gate_probs: float32 [128, 2], P(('gy', 'gz')), may hold values from 0.2 to 1
- gate_weight: bfloat16 [8, 4096, 16384], P('gy', None, ('gz', 'gx')), may hold values from -0.09375 to 0.09375
- up_weight: bfloat16 [8, 4096, 16384], P('gy', None, ('gz', 'gx')), may hold values from -0.09375 to 0.09375
- down_weight: bfloat16 [8, 16384, 4096], P('gy', 'gz', 'gx'), may hold values from -0.046875 to 0.046875
Outputs:
- moe_output: bfloat16 [128, 4096], P(('gy', 'gz'), 'gx')
The draws below stay inside these ranges and needn't reach their ends.
Inputs may be any that keep to these rules, and one draw needn't show every extreme that they name: `expert_ids`: A token's two ids differ. Within each aligned block of 16 tokens no expert is named more than 8 times, and in some blocks one expert is named exactly 8 times.
All inputs are finite; a program needn't handle non-finite values.
Results may differ from the reference program's by a relative error of at most 0.0049.
Values may be sent and summed in bfloat16 or wider, within the bound.
A program may use at most 192 MiB of HBM per device.

```python
import math
import jax
import jax.numpy as jnp
import numpy as np
from jax import lax

D = 4096
FF = 16384
EXPERTS = 8
TOK_DEV = 16
CAP = 8
TOKENS = 128
SLOTS = 64


def steps_of(key, extent, pieces, low, largest):
    loudness, own = 1.0, jax.random.fold_in(key, 6)
    for position, blocks in pieces:
        heights = jnp.exp(jax.random.uniform(jax.random.fold_in(own, position), (blocks,), jnp.float32, low / len(pieces), largest / len(pieces)))
        loudness = loudness * jnp.repeat(heights, extent[position] // blocks).reshape([-1 if axis == position else 1 for axis in range(len(extent))])
    return loudness


def deal_out(rng, own, number, rows, amount, top, limit, slope):
    sequence = jax.random.permutation(rng, amount)
    crowded, usual = load_shares(amount, rows * top, limit, slope, True), load_shares(amount, rows * top, limit, slope, False)
    places = jnp.arange(amount)

    def named(tallies, rotation):
        used = int((tallies > 0).sum())
        fixed = max(1, used // 4)
        shifted = fixed + (places - fixed + rotation * (used - fixed)) % max(1, amount - fixed)
        return jnp.zeros((amount,), jnp.int32).at[sequence[jnp.where(places < fixed, places, shifted)]].set(jnp.asarray(tallies, jnp.int32))

    tallies = jnp.where(number % 4 == 0, named(crowded, number // 4), named(usual, number - number // 4 - 1))
    mixed = jax.random.permutation(jax.random.fold_in(own, 3), amount)
    donor, sink = mixed[0:amount // 2 * 2:2], mixed[1:amount // 2 * 2:2]
    room = jnp.minimum(tallies[donor] - 1, limit - tallies[sink]) // 2
    room = jnp.where((donor == sequence[0]) | (sink == sequence[0]) | (tallies[sink] == 0), 0, jnp.maximum(room, 0))
    shifted = jax.random.randint(jax.random.fold_in(own, 4), (amount // 2,), 0, 1 << 20) % (room + 1)
    tallies = tallies.at[donor].add(-shifted).at[sink].add(shifted)
    members = jnp.searchsorted(jnp.cumsum(tallies), jnp.arange(rows * top), side="right").astype(jnp.int32)
    listing = members.reshape(top, rows).T
    listing = listing[jax.random.permutation(jax.random.fold_in(own, 1), rows)]
    rotation = jax.random.randint(jax.random.fold_in(own, 2), (rows, 1), 0, top)
    return jnp.take_along_axis(listing, (jnp.arange(top)[None, :] + rotation) % top, axis=1)


def load_shares(amount, total, bound, slope, full):
    weights = [(1 << 20) // math.isqrt(rank ** slope) + 1 for rank in range(1, amount + 1)]
    largest = bound if full else min(bound, max(-(-total // amount), total * weights[0] // sum(weights)))
    least = 1 if total - largest >= amount - 1 else 0
    holding, surplus = [largest] + [least] * (amount - 1), total - largest - least * (amount - 1)
    while surplus > 0:
        free = [i for i in range(1, amount) if holding[i] < largest] or [i for i in range(1, amount) if holding[i] < bound]
        pool, remaining = sum([weights[i] for i in free]), surplus
        for i in free:
            addition = min(bound - holding[i], max(1, remaining * weights[i] // pool), surplus)
            holding[i] = holding[i] + addition
            surplus = surplus - addition
    return np.array(holding)


def scatter_about(own_key, dims, spread, reach, pieces=(), kind=jnp.bfloat16):
    array = spread * jax.random.normal(own_key, dims, jnp.float32)
    if pieces:
        array = array * steps_of(own_key, dims, pieces, -0.22, 0.18)
    return jnp.clip(array, -reach, reach).astype(kind)


def setup_inputs(seed: int = 0) -> dict:
    seeds = jax.random.split(jax.random.key(seed), 7)
    tokens = scatter_about(seeds[0], (TOKENS, D), 1.0, 6.0, ((0, 8), (1, 4)))
    expert_ids_keys = jax.random.split(jax.random.fold_in(seeds[1], 1), TOKENS // TOK_DEV)
    expert_ids_turns = jax.random.permutation(jax.random.fold_in(seeds[1], 3), TOKENS // TOK_DEV)
    expert_ids = jax.vmap(lambda own, number: deal_out(jax.random.fold_in(seeds[1], 2), own, number, TOK_DEV, EXPERTS, 2, CAP, 2))(expert_ids_keys, expert_ids_turns).reshape((TOKENS, 2))
    gate_probs = jnp.clip(0.2 + 0.8 * jax.random.uniform(seeds[2], (TOKENS, 2), jnp.float32) ** steps_of(seeds[2], (TOKENS, 2), ((0, 8),), -0.2, 0.2), 0.2, 1.0)
    gate_weight = scatter_about(seeds[3], (EXPERTS, D, FF), D ** -0.5, 0.09375, ((0, 2), (2, 16)))
    up_weight = scatter_about(seeds[4], (EXPERTS, D, FF), D ** -0.5, 0.09375, ((0, 2), (2, 16)))
    down_weight = scatter_about(seeds[5], (EXPERTS, FF, D), FF ** -0.5, 0.046875, ((0, 2), (1, 4), (2, 4)))
    return dict(tokens=tokens, expert_ids=expert_ids, gate_probs=gate_probs, gate_weight=gate_weight, up_weight=up_weight, down_weight=down_weight)


def slot_numbers(expert_ids):
    grouped = expert_ids.reshape(-1, 2 * TOK_DEV)
    labels = jnp.arange(EXPERTS, dtype=jnp.int32)
    onehot = (grouped[:, :, None] == labels[None, None, :]).astype(jnp.int32)
    before = jnp.cumsum(onehot, axis=1) - onehot
    slot_index = jnp.sum(before * onehot, axis=2)
    return slot_index.reshape(-1, 2).astype(jnp.int32)


def reference(tokens, expert_ids, gate_probs, gate_weight, up_weight, down_weight):
    slot_index = slot_numbers(expert_ids)
    owner_row = (jnp.arange(TOKENS, dtype=jnp.int32) // TOK_DEV)[:, None]
    places = owner_row * CAP + slot_index
    columns = jnp.arange(SLOTS, dtype=jnp.int32)

    def one_expert(running, expert):
        chosen = expert_ids == expert
        matches = chosen[:, :, None] & (places[:, :, None] == columns[None, None, :])
        matches = matches.astype(jnp.float32)
        picker = jnp.sum(matches, axis=1)
        combine_table = jnp.sum(matches * gate_probs[:, :, None], axis=1)
        buffer = jnp.dot(picker.T.astype(jnp.bfloat16), tokens, preferred_element_type=jnp.float32).astype(jnp.bfloat16)
        gate_act = jnp.dot(buffer, gate_weight[expert], preferred_element_type=jnp.float32)
        up_act = jnp.dot(buffer, up_weight[expert], preferred_element_type=jnp.float32)
        hidden = (jax.nn.silu(gate_act) * up_act).astype(jnp.bfloat16)
        expert_out = jnp.dot(hidden, down_weight[expert], preferred_element_type=jnp.float32)
        added = jnp.dot(combine_table, expert_out, precision=lax.Precision.HIGHEST, preferred_element_type=jnp.float32)
        return running + added, None

    running, _ = lax.scan(one_expert, jnp.zeros((TOKENS, D), jnp.float32), jnp.arange(EXPERTS, dtype=jnp.int32))
    return running.astype(jnp.bfloat16)
```

```python
import functools

import jax
import jax.numpy as jnp
from jax import lax
from jax.experimental import pallas as pl
from jax.experimental.pallas import tpu as pltpu
from jax.sharding import PartitionSpec as P

EXPERTS = 8
CAP = 8
MESH = pl.DeviceIdType.MESH
LAG = 2
F32 = jnp.float32
BF16 = jnp.bfloat16


def kernel(
    dims,
    tok_ref,
    info_ref,
    gate_hbm,
    up_hbm,
    down_hbm,
    out_ref,
    ring,
    tokbuf,
    infobuf,
    buf,
    pick,
    pick_t,
    scale,
    hid,
    yhi,
    ylo,
    part,
    parts,
    wsem,
    info_s,
    info_r,
    gx_s,
    gx_r,
    a1_s,
    a1_r,
    a2_s,
    a2_r,
    b1_s,
    b1_r,
    b2_s,
    b2_r,
    core_sem,
    up_s,
    dn_s,
    hid_r,
    out_s,
    out_r,
):
    G, Y, X, C, EL, TOK, W, D, HC, HR, WO, cw, NS = dims
    Z = X * C
    NB = Y * Z
    T = NB * TOK
    R = NB * CAP
    NJ, ND = HC // cw, WO // cw
    U = EL * NJ
    NC = 2 * U + EL * ND
    gx, gy, gz = lax.axis_index("gx"), lax.axis_index("gy"), lax.axis_index("gz")
    cx, cc = gz // C, lax.rem(gz, C)
    block = gy * Z + gz

    def start_gate(u, c):
        j, n = u // NJ, lax.rem(u, NJ)
        cols = pl.ds(pl.multiple_of(n * cw, cw), cw)
        slot = lax.rem(c, NS)
        pltpu.make_async_copy(
            gate_hbm.at[j, :, cols], ring.at[slot, pl.ds(0, D)], wsem.at[slot]
        ).start()

    def start_up(u, c):
        j, n = u // NJ, lax.rem(u, NJ)
        cols = pl.ds(pl.multiple_of(n * cw, cw), cw)
        slot = lax.rem(c, NS)
        pltpu.make_async_copy(
            up_hbm.at[j, :, cols], ring.at[slot, pl.ds(0, D)], wsem.at[slot]
        ).start()

    def start_down(q, c):
        j, n = q // ND, lax.rem(q, ND)
        cols = pl.ds(pl.multiple_of(n * cw, cw), cw)
        slot = lax.rem(c, NS)
        pltpu.make_async_copy(
            down_hbm.at[j, :, cols], ring.at[slot, pl.ds(0, HR)], wsem.at[slot]
        ).start()

    def start_chunk(c):
        gated = c < 2 * U

        @pl.when(jnp.logical_and(gated, lax.rem(c, 2) == 0))
        def _():
            start_gate(c // 2, c)

        @pl.when(jnp.logical_and(gated, lax.rem(c, 2) == 1))
        def _():
            start_up(c // 2, c)

        @pl.when(jnp.logical_and(c >= 2 * U, c < NC))
        def _():
            start_down(c - 2 * U, c)

    def wait_chunk(c, rows):
        slot = lax.rem(c, NS)
        pltpu.make_async_copy(
            ring.at[slot, pl.ds(0, rows)], ring.at[slot, pl.ds(0, rows)], wsem.at[slot]
        ).wait()
        return slot

    lax.fori_loop(0, NS, lambda c, _: (start_chunk(c), 0)[1], 0)

    barrier = pltpu.get_barrier_semaphore()
    for d in range(1, G):
        pl.semaphore_signal(
            barrier, inc=1, device_id={"gx": lax.rem(gx + d, G)}, device_id_type=MESH
        )

    def plane(b):
        return {"gy": b // Z, "gz": lax.rem(b, Z)}

    for d in range(1, NB):
        pl.semaphore_signal(
            barrier, inc=1, device_id=plane(lax.rem(block + d, NB)), device_id_type=MESH
        )
    pl.semaphore_wait(barrier, G - 1 + NB - 1)

    def remote(src, dst, ssem, rsem, device):
        return pltpu.make_async_remote_copy(
            src_ref=src, dst_ref=dst, send_sem=ssem, recv_sem=rsem,
            device_id=device, device_id_type=MESH,
        )

    def ring_copies(n, me, axis_device, src, dst, ssem, rsem):
        copies = []
        for d in range(1, n):
            peer = lax.rem(me + d, n)
            copies.append(remote(src, dst(me), ssem.at[d], rsem.at[me], axis_device(peer)))
        return copies

    def wait_from(n, me, dst, rsem, ssem, axis_device):
        for d in range(1, n):
            peer = lax.rem(me + d, n)
            remote(dst(peer), dst(peer), ssem.at[d], rsem.at[peer], axis_device(peer)).wait_recv()

    on_gx = lambda i: {"gx": i}
    on_gy = lambda i: {"gy": i}
    on_x = lambda i: {"gz": i * C + cc}

    def tok_at(i):
        return tokbuf.at[i, gy, cx, cc]

    gx_copies = ring_copies(G, gx, on_gx, tok_ref, tok_at, gx_s, gx_r)
    for c in gx_copies:
        c.start()

    def info_at(b):
        return infobuf.at[b]

    info_copies = ring_copies(NB, block, plane, info_ref, info_at, info_s, info_r)
    for c in info_copies:
        c.start()
    tokbuf[gx, gy, cx, cc] = tok_ref[...]
    infobuf[block] = info_ref[...]

    H = G // 2
    low, high = pl.ds(0, H), pl.ds(H, G - H)
    wait_from(G, gx, tok_at, gx_r, gx_s, on_gx)

    a1_at = lambda i: tokbuf.at[low, i, cx, cc]
    b1_at = lambda i: tokbuf.at[high, gy, i, cc]
    a2_at = lambda i: tokbuf.at[low, :, i, cc]
    b2_at = lambda i: tokbuf.at[high, i, :, cc]
    a1 = ring_copies(Y, gy, on_gy, a1_at(gy), a1_at, a1_s, a1_r)
    b1 = ring_copies(X, cx, on_x, b1_at(cx), b1_at, b1_s, b1_r)
    for c in a1 + b1:
        c.start()

    wait_from(NB, block, info_at, info_r, info_s, plane)
    info_t = infobuf[...].reshape(T, 128).T
    id0, id1 = info_t[0:1], info_t[1:2]
    p0, p1 = info_t[2:3], info_t[3:4]
    first = (gy * EL).astype(F32)
    chosen = [
        jnp.where(id0 == first + j, 1.0, 0.0) + jnp.where(id1 == first + j, 1.0, 0.0)
        for j in range(EL)
    ]
    padded = chosen + [jnp.zeros((1, T), F32)] * (-EL % 16)
    t2 = lax.broadcasted_iota(jnp.int32, (T, T), 0)
    t1 = lax.broadcasted_iota(jnp.int32, (T, T), 1)
    earlier = jnp.where((t2 < t1) & (t2 // TOK == t1 // TOK), 1.0, 0.0).astype(BF16)
    before = jnp.dot(
        jnp.concatenate(padded, axis=0).astype(BF16), earlier, preferred_element_type=F32
    )
    base = (lax.broadcasted_iota(jnp.int32, (1, T), 1) // TOK * CAP).astype(F32)
    rows = lax.broadcasted_iota(jnp.int32, (R, T), 0).astype(F32)
    tables = []
    for j in range(EL):
        target = jnp.where(chosen[j] > 0.5, base + before[j:j + 1], -1.0)
        table = jnp.where(rows == target, 1.0, 0.0)
        prob = jnp.where(id0 == first + j, p0, p1)
        scale[j * R:(j + 1) * R] = jnp.sum(table * prob, axis=1, keepdims=True)
        tables.append(table)
    table = jnp.concatenate(tables, axis=0)
    pick[...] = table.astype(BF16)
    pick_t[...] = table.T.astype(BF16)

    wait_from(Y, gy, a1_at, a1_r, a1_s, on_gy)
    a2 = ring_copies(X, cx, on_x, a2_at(cx), a2_at, a2_s, a2_r)
    for c in a2:
        c.start()
    wait_from(X, cx, b1_at, b1_r, b1_s, on_x)
    b2 = ring_copies(Y, gy, on_gy, b2_at(gy), b2_at, b2_s, b2_r)
    for c in b2:
        c.start()
    core_copies = []
    for half, (part_g, wait) in enumerate(
        (
            (low, lambda: wait_from(X, cx, a2_at, a2_r, a2_s, on_x)),
            (high, lambda: wait_from(Y, gy, b2_at, b2_r, b2_s, on_gy)),
        )
    ):
        wait()
        other = 1 - cc
        c = remote(
            tokbuf.at[part_g, :, :, cc], tokbuf.at[part_g, :, :, cc],
            core_sem.at[0, half], core_sem.at[1, half], {"gz": cx * C + other},
        )
        c.start()
        core_copies.append(c)
    for half, (c, lo, hi) in enumerate(((core_copies[0], 0, H), (core_copies[1], H, G))):
        c.wait_recv()
        for g in range(lo, hi):
            rows_g = tokbuf[g].reshape(T, W)
            buf[:, g * W:(g + 1) * W] = jnp.dot(
                pick[...], rows_g, preferred_element_type=F32
            ).astype(BF16)

    def hop(u, s, step, sem):
        return remote(
            hid.at[u, s], hid.at[u, s], sem.at[u, s], hid_r.at[u, s],
            {"gx": jnp.clip(gx + step, 0, G - 1)},
        )

    def send_up(u, s):
        @pl.when(gx < G - 1)
        def _():
            hop(u, s, 1, up_s).start()

    def send_down(u, s):
        @pl.when(gx > 0)
        def _():
            hop(u, s, -1, dn_s).start()

    def relay(t):
        for d in range(1, G):
            v = t - LAG * d
            s = gx - d
            live = jnp.logical_and(v >= 0, v < U)

            @pl.when(jnp.logical_and(live, s >= 0))
            def _():
                hop(v, s, -1, dn_s).wait_recv()
                send_up(v, s)

            r = gx + d

            @pl.when(jnp.logical_and(live, r < G))
            def _():
                hop(v, r, 1, up_s).wait_recv()
                send_down(v, r)

    def unit(u):
        j = u // NJ
        x = buf[pl.ds(pl.multiple_of(j * R, R), R), :]
        sg = wait_chunk(2 * u, D)
        gate = jnp.dot(x, ring[sg, pl.ds(0, D), :], preferred_element_type=F32)
        su = wait_chunk(2 * u + 1, D)
        up = jnp.dot(x, ring[su, pl.ds(0, D), :], preferred_element_type=F32)
        hid[u, gx] = (gate / (1.0 + jnp.exp(-gate)) * up).astype(BF16)
        send_up(u, gx)
        send_down(u, gx)
        start_chunk(2 * u + NS)
        start_chunk(2 * u + 1 + NS)

    def step(t, _):
        relay(t)
        unit(t)
        return 0

    lax.fori_loop(0, U, step, 0)

    def down(q):
        j, n = q // ND, lax.rem(q, ND)
        c = 2 * U + q
        slot = wait_chunk(c, HR)
        x = jnp.concatenate(
            [hid[j * NJ + v, s] for s in range(G) for v in range(NJ)], axis=1
        )
        acc = jnp.dot(x, ring[slot, pl.ds(0, HR), :], preferred_element_type=F32)
        start_chunk(c + NS)
        at = pl.ds(pl.multiple_of(j * R, R), R)
        y = acc * scale[at]
        top = y.astype(BF16)
        yhi[n, at] = top
        ylo[n, at] = (y - top.astype(F32)).astype(BF16)

    drain = LAG * (G - 1)
    early = (EL - 1) * ND
    per = -(-early // drain) if early else 0
    fits = all(
        U + q // per >= (q // ND + 1) * NJ - 1 + drain for q in range(early)
    ) if early else True

    def drain_step(i, _):
        relay(U + i)
        for k in range(per if fits else 0):
            q = i * per + k

            @pl.when(q < early)
            def _():
                down(q)

        return 0

    lax.fori_loop(0, drain, drain_step, 0)
    if not fits:
        lax.fori_loop(0, early, lambda q, _: (down(q), 0)[1], 0)

    def give(n, d):
        b = lax.rem(block + d, NB)
        return remote(
            part.at[n, b], parts.at[n, block], out_s.at[n, d], out_r.at[n, block], plane(b)
        )

    def last(n, _):
        down(early + n)
        both = jnp.dot(pick_t[...], yhi[n], preferred_element_type=F32) + jnp.dot(
            pick_t[...], ylo[n], preferred_element_type=F32
        )
        part[n] = both.astype(BF16).reshape(NB, TOK, cw)
        for d in range(1, NB):
            give(n, d).start()
        parts[n, block] = part[n, block]
        return 0

    lax.fori_loop(0, ND, last, 0)

    for n in range(ND):
        for d in range(1, NB):
            b = lax.rem(block + d, NB)
            remote(
                parts.at[n, b], parts.at[n, b], out_s.at[n, d], out_r.at[n, b], plane(b)
            ).wait_recv()
        total = parts[n, 0].astype(F32)
        for b in range(1, NB):
            total = total + parts[n, b].astype(F32)
        out_ref[:, n * cw:(n + 1) * cw] = total.astype(BF16)

    for c in gx_copies + info_copies + a1 + b1 + a2 + b2 + core_copies:
        c.wait_send()

    def settle(u, _):
        for s in range(G):
            @pl.when(jnp.logical_and(gx < G - 1, s <= gx))
            def _():
                hop(u, s, 1, up_s).wait_send()

            @pl.when(jnp.logical_and(gx > 0, s >= gx))
            def _():
                hop(u, s, -1, dn_s).wait_send()

        return 0

    lax.fori_loop(0, U, settle, 0)
    for n in range(ND):
        for d in range(1, NB):
            give(n, d).wait_send()


def body(sizes, tokens, expert_ids, gate_probs, gate_weight, up_weight, down_weight):
    G, Y, Z = sizes
    C = 2
    X = Z // C
    NB = Y * Z
    EL, D, HC = gate_weight.shape
    _, HR, WO = down_weight.shape
    TOK, W = tokens.shape
    cw = min(256, HC, WO)
    T, R = NB * TOK, NB * CAP
    NJ, ND = HC // cw, WO // cw
    U = EL * NJ
    NC = 2 * U + EL * ND
    deep = max(D, HR)
    NS = min(NC, (46 << 20) // (deep * cw * 2)) // 2 * 2
    info = jnp.concatenate(
        [expert_ids.astype(F32), gate_probs, jnp.zeros((TOK, 124), F32)], axis=1
    )
    dims = (G, Y, X, C, EL, TOK, W, D, HC, HR, WO, cw, NS)
    dma = pltpu.SemaphoreType.DMA
    vmem = pl.BlockSpec(memory_space=pltpu.VMEM)
    hbm = pl.BlockSpec(memory_space=pl.ANY)
    return pl.pallas_call(
        functools.partial(kernel, dims),
        out_shape=jax.ShapeDtypeStruct((TOK, WO), BF16),
        in_specs=[vmem, vmem, hbm, hbm, hbm],
        out_specs=vmem,
        scratch_shapes=[
            pltpu.VMEM((NS, deep, cw), BF16),
            pltpu.VMEM((G, Y, X, C, TOK, W), BF16),
            pltpu.VMEM((NB, TOK, 128), F32),
            pltpu.VMEM((EL * R, D), BF16),
            pltpu.VMEM((EL * R, T), BF16),
            pltpu.VMEM((T, EL * R), BF16),
            pltpu.VMEM((EL * R, 1), F32),
            pltpu.VMEM((U, G, R, cw), BF16),
            pltpu.VMEM((ND, EL * R, cw), BF16),
            pltpu.VMEM((ND, EL * R, cw), BF16),
            pltpu.VMEM((ND, NB, TOK, cw), BF16),
            pltpu.VMEM((ND, NB, TOK, cw), BF16),
            dma((NS,)),
            dma((NB,)), dma((NB,)),
            dma((G,)), dma((G,)),
            dma((Y,)), dma((Y,)),
            dma((X,)), dma((X,)),
            dma((X,)), dma((X,)),
            dma((Y,)), dma((Y,)),
            dma((2, 2)),
            dma((U, G)), dma((U, G)), dma((U, G)),
            dma((ND, NB)), dma((ND, NB)),
        ],
        compiler_params=pltpu.CompilerParams(
            collective_id=0, has_side_effects=True, vmem_limit_bytes=60 << 20
        ),
        cost_estimate=pl.CostEstimate(
            flops=2 * EL * R * (2 * D * HC + HR * WO),
            bytes_accessed=2 * EL * (2 * D * HC + HR * WO),
            transcendentals=EL * R * HC,
        ),
    )(tokens, info, gate_weight, up_weight, down_weight)


def solution(mesh):
    sizes = (mesh.shape["gx"], mesh.shape["gy"], mesh.shape["gz"])
    return jax.shard_map(
        functools.partial(body, sizes),
        mesh=mesh,
        in_specs=(
            P(("gy", "gz"), "gx"),
            P(("gy", "gz"), None),
            P(("gy", "gz"), None),
            P("gy", None, ("gz", "gx")),
            P("gy", None, ("gz", "gx")),
            P("gy", "gz", "gx"),
        ),
        out_specs=P(("gy", "gz"), "gx"),
        check_vma=False,
    )
```

```python
import functools

import jax
import jax.numpy as jnp
from jax import lax
from jax.experimental import pallas as pl
from jax.experimental.pallas import tpu as pltpu
from jax.sharding import PartitionSpec as P

EXPERTS = 8
CAP = 8
MESH = pl.DeviceIdType.MESH
LAG = 3
F32 = jnp.float32
BF16 = jnp.bfloat16


def kernel(
    dims,
    tok_ref,
    info_ref,
    gate_hbm,
    up_hbm,
    down_hbm,
    out_ref,
    ring,
    tokbuf,
    infobuf,
    buf,
    pick,
    pick_t,
    scale,
    hid,
    yhi,
    ylo,
    part,
    parts,
    wsem,
    info_s,
    info_r,
    gx_s,
    gx_r,
    a1_s,
    a1_r,
    a2_s,
    a2_r,
    b1_s,
    b1_r,
    b2_s,
    b2_r,
    core_sem,
    up_s,
    dn_s,
    hid_r,
    out_s,
    out_r,
):
    G, Y, X, C, EL, TOK, W, D, HC, HR, WO, cw, NS = dims
    Z = X * C
    NB = Y * Z
    T = NB * TOK
    R = NB * CAP
    NJ, ND = HC // cw, WO // cw
    U = EL * NJ
    NC = 2 * U + EL * ND
    gx, gy, gz = lax.axis_index("gx"), lax.axis_index("gy"), lax.axis_index("gz")
    cx, cc = gz // C, lax.rem(gz, C)
    block = gy * Z + gz

    def start_gate(u, c):
        j, n = u // NJ, lax.rem(u, NJ)
        cols = pl.ds(pl.multiple_of(n * cw, cw), cw)
        slot = lax.rem(c, NS)
        pltpu.make_async_copy(
            gate_hbm.at[j, :, cols], ring.at[slot, pl.ds(0, D)], wsem.at[slot]
        ).start()

    def start_up(u, c):
        j, n = u // NJ, lax.rem(u, NJ)
        cols = pl.ds(pl.multiple_of(n * cw, cw), cw)
        slot = lax.rem(c, NS)
        pltpu.make_async_copy(
            up_hbm.at[j, :, cols], ring.at[slot, pl.ds(0, D)], wsem.at[slot]
        ).start()

    def start_down(q, c):
        j, n = q // ND, lax.rem(q, ND)
        cols = pl.ds(pl.multiple_of(n * cw, cw), cw)
        slot = lax.rem(c, NS)
        pltpu.make_async_copy(
            down_hbm.at[j, :, cols], ring.at[slot, pl.ds(0, HR)], wsem.at[slot]
        ).start()

    def start_chunk(c):
        gated = c < 2 * U

        @pl.when(jnp.logical_and(gated, lax.rem(c, 2) == 0))
        def _():
            start_gate(c // 2, c)

        @pl.when(jnp.logical_and(gated, lax.rem(c, 2) == 1))
        def _():
            start_up(c // 2, c)

        @pl.when(jnp.logical_and(c >= 2 * U, c < NC))
        def _():
            start_down(c - 2 * U, c)

    def wait_chunk(c, rows):
        slot = lax.rem(c, NS)
        pltpu.make_async_copy(
            ring.at[slot, pl.ds(0, rows)], ring.at[slot, pl.ds(0, rows)], wsem.at[slot]
        ).wait()
        return slot

    lax.fori_loop(0, NS, lambda c, _: (start_chunk(c), 0)[1], 0)

    barrier = pltpu.get_barrier_semaphore()
    for d in range(1, G):
        pl.semaphore_signal(
            barrier, inc=1, device_id={"gx": lax.rem(gx + d, G)}, device_id_type=MESH
        )

    def plane(b):
        return {"gy": b // Z, "gz": lax.rem(b, Z)}

    for d in range(1, NB):
        pl.semaphore_signal(
            barrier, inc=1, device_id=plane(lax.rem(block + d, NB)), device_id_type=MESH
        )
    pl.semaphore_wait(barrier, G - 1 + NB - 1)

    def remote(src, dst, ssem, rsem, device):
        return pltpu.make_async_remote_copy(
            src_ref=src, dst_ref=dst, send_sem=ssem, recv_sem=rsem,
            device_id=device, device_id_type=MESH,
        )

    def ring_copies(n, me, axis_device, src, dst, ssem, rsem):
        copies = []
        for d in range(1, n):
            peer = lax.rem(me + d, n)
            copies.append(remote(src, dst(me), ssem.at[d], rsem.at[me], axis_device(peer)))
        return copies

    def wait_from(n, me, dst, rsem, ssem, axis_device):
        for d in range(1, n):
            peer = lax.rem(me + d, n)
            remote(dst(peer), dst(peer), ssem.at[d], rsem.at[peer], axis_device(peer)).wait_recv()

    on_gx = lambda i: {"gx": i}
    on_gy = lambda i: {"gy": i}
    on_x = lambda i: {"gz": i * C + cc}

    def tok_at(i):
        return tokbuf.at[i, gy, cx, cc]

    gx_copies = ring_copies(G, gx, on_gx, tok_ref, tok_at, gx_s, gx_r)
    for c in gx_copies:
        c.start()

    def info_at(b):
        return infobuf.at[b]

    info_copies = ring_copies(NB, block, plane, info_ref, info_at, info_s, info_r)
    for c in info_copies:
        c.start()
    tokbuf[gx, gy, cx, cc] = tok_ref[...]
    infobuf[block] = info_ref[...]

    H = G // 2
    low, high = pl.ds(0, H), pl.ds(H, G - H)
    wait_from(G, gx, tok_at, gx_r, gx_s, on_gx)

    a1_at = lambda i: tokbuf.at[low, i, cx, cc]
    b1_at = lambda i: tokbuf.at[high, gy, i, cc]
    a2_at = lambda i: tokbuf.at[low, :, i, cc]
    b2_at = lambda i: tokbuf.at[high, i, :, cc]
    a1 = ring_copies(Y, gy, on_gy, a1_at(gy), a1_at, a1_s, a1_r)
    b1 = ring_copies(X, cx, on_x, b1_at(cx), b1_at, b1_s, b1_r)
    for c in a1 + b1:
        c.start()

    wait_from(NB, block, info_at, info_r, info_s, plane)
    info_t = infobuf[...].reshape(T, 128).T
    id0, id1 = info_t[0:1], info_t[1:2]
    first = (gy * EL).astype(F32)
    chosen = [
        jnp.where(id0 == first + j, 1.0, 0.0) + jnp.where(id1 == first + j, 1.0, 0.0)
        for j in range(EL)
    ]
    padded = chosen + [jnp.zeros((1, T), F32)] * (-EL % 16)
    t2 = lax.broadcasted_iota(jnp.int32, (T, T), 0)
    t1 = lax.broadcasted_iota(jnp.int32, (T, T), 1)
    earlier = jnp.where((t2 < t1) & (t2 // TOK == t1 // TOK), 1.0, 0.0).astype(BF16)
    before = jnp.dot(
        jnp.concatenate(padded, axis=0).astype(BF16), earlier, preferred_element_type=F32
    )
    base = (lax.broadcasted_iota(jnp.int32, (1, T), 1) // TOK * CAP).astype(F32)
    rows = lax.broadcasted_iota(jnp.int32, (R, T), 0).astype(F32)
    tables = []
    for j in range(EL):
        target = jnp.where(chosen[j] > 0.5, base + before[j:j + 1], -1.0)
        table = jnp.where(rows == target, 1.0, 0.0)
        tables.append(table)
    pick[...] = jnp.concatenate(tables, axis=0).astype(BF16)

    wait_from(Y, gy, a1_at, a1_r, a1_s, on_gy)
    a2 = ring_copies(X, cx, on_x, a2_at(cx), a2_at, a2_s, a2_r)
    for c in a2:
        c.start()
    wait_from(X, cx, b1_at, b1_r, b1_s, on_x)
    b2 = ring_copies(Y, gy, on_gy, b2_at(gy), b2_at, b2_s, b2_r)
    for c in b2:
        c.start()
    core_copies = []
    for half, (part_g, wait) in enumerate(
        (
            (low, lambda: wait_from(X, cx, a2_at, a2_r, a2_s, on_x)),
            (high, lambda: wait_from(Y, gy, b2_at, b2_r, b2_s, on_gy)),
        )
    ):
        wait()
        other = 1 - cc
        c = remote(
            tokbuf.at[part_g, :, :, cc], tokbuf.at[part_g, :, :, cc],
            core_sem.at[0, half], core_sem.at[1, half], {"gz": cx * C + other},
        )
        c.start()
        core_copies.append(c)
    for c in core_copies:
        c.wait_recv()

    def fill(j):
        at = pl.ds(pl.multiple_of(j * R, R), R)
        for g in range(G):
            buf[at, g * W:(g + 1) * W] = jnp.dot(
                pick[at], tokbuf[g].reshape(T, W), preferred_element_type=F32
            ).astype(BF16)

    def hop(u, s, step, sem):
        return remote(
            hid.at[u, s], hid.at[u, s], sem.at[u, s], hid_r.at[u, s],
            {"gx": jnp.clip(gx + step, 0, G - 1)},
        )

    def send_up(u, s):
        @pl.when(gx < G - 1)
        def _():
            hop(u, s, 1, up_s).start()

    def send_down(u, s):
        @pl.when(gx > 0)
        def _():
            hop(u, s, -1, dn_s).start()

    def relay(t):
        for d in range(1, G):
            v = t - LAG * d
            s = gx - d
            live = jnp.logical_and(v >= 0, v < U)

            @pl.when(jnp.logical_and(live, s >= 0))
            def _():
                hop(v, s, -1, dn_s).wait_recv()
                send_up(v, s)

            r = gx + d

            @pl.when(jnp.logical_and(live, r < G))
            def _():
                hop(v, r, 1, up_s).wait_recv()
                send_down(v, r)

    def unit(u):
        j = u // NJ

        @pl.when(lax.rem(u, NJ) == 0)
        def _():
            fill(j)

        x = buf[pl.ds(pl.multiple_of(j * R, R), R), :]
        sg = wait_chunk(2 * u, D)
        gate = jnp.dot(x, ring[sg, pl.ds(0, D), :], preferred_element_type=F32)
        su = wait_chunk(2 * u + 1, D)
        up = jnp.dot(x, ring[su, pl.ds(0, D), :], preferred_element_type=F32)
        hid[u, gx] = (gate / (1.0 + jnp.exp(-gate)) * up).astype(BF16)
        send_up(u, gx)
        send_down(u, gx)
        start_chunk(2 * u + NS)
        start_chunk(2 * u + 1 + NS)

    def step(t, _):
        relay(t)
        unit(t)
        return 0

    lax.fori_loop(0, U, step, 0)

    pick_t[...] = pick[...].astype(F32).T.astype(BF16)
    probs_t = infobuf[...].reshape(T, 128).T
    for j in range(EL):
        prob = jnp.where(probs_t[0:1] == first + j, probs_t[2:3], probs_t[3:4])
        scale[j * R:(j + 1) * R] = jnp.sum(
            pick[j * R:(j + 1) * R].astype(F32) * prob, axis=1, keepdims=True
        )

    def down(q):
        j, n = q // ND, lax.rem(q, ND)
        c = 2 * U + q
        slot = wait_chunk(c, HR)
        x = jnp.concatenate(
            [hid[j * NJ + v, s] for s in range(G) for v in range(NJ)], axis=1
        )
        acc = jnp.dot(x, ring[slot, pl.ds(0, HR), :], preferred_element_type=F32)
        start_chunk(c + NS)
        at = pl.ds(pl.multiple_of(j * R, R), R)
        y = acc * scale[at]
        top = y.astype(BF16)
        yhi[n, at] = top
        ylo[n, at] = (y - top.astype(F32)).astype(BF16)

    drain = LAG * (G - 1)
    early = (EL - 1) * ND
    per = -(-early // drain) if early else 0
    fits = all(
        U + q // per >= (q // ND + 1) * NJ - 1 + drain for q in range(early)
    ) if early else True

    def drain_step(i, _):
        relay(U + i)
        for k in range(per if fits else 0):
            q = i * per + k

            @pl.when(q < early)
            def _():
                down(q)

        return 0

    lax.fori_loop(0, drain, drain_step, 0)
    if not fits:
        lax.fori_loop(0, early, lambda q, _: (down(q), 0)[1], 0)

    def give(n, d):
        b = lax.rem(block + d, NB)
        return remote(
            part.at[n, b], parts.at[n, block], out_s.at[n, d], out_r.at[n, block], plane(b)
        )

    def last(n, _):
        down(early + n)
        both = jnp.dot(pick_t[...], yhi[n], preferred_element_type=F32) + jnp.dot(
            pick_t[...], ylo[n], preferred_element_type=F32
        )
        part[n] = both.astype(BF16).reshape(NB, TOK, cw)
        for d in range(1, NB):
            give(n, d).start()
        parts[n, block] = part[n, block]
        return 0

    lax.fori_loop(0, ND, last, 0)

    for n in range(ND):
        for d in range(1, NB):
            b = lax.rem(block + d, NB)
            remote(
                parts.at[n, b], parts.at[n, b], out_s.at[n, d], out_r.at[n, b], plane(b)
            ).wait_recv()
        total = parts[n, 0].astype(F32)
        for b in range(1, NB):
            total = total + parts[n, b].astype(F32)
        out_ref[:, n * cw:(n + 1) * cw] = total.astype(BF16)

    for c in gx_copies + info_copies + a1 + b1 + a2 + b2 + core_copies:
        c.wait_send()

    def settle(u, _):
        for s in range(G):
            @pl.when(jnp.logical_and(gx < G - 1, s <= gx))
            def _():
                hop(u, s, 1, up_s).wait_send()

            @pl.when(jnp.logical_and(gx > 0, s >= gx))
            def _():
                hop(u, s, -1, dn_s).wait_send()

        return 0

    lax.fori_loop(0, U, settle, 0)
    for n in range(ND):
        for d in range(1, NB):
            give(n, d).wait_send()


def body(sizes, tokens, expert_ids, gate_probs, gate_weight, up_weight, down_weight):
    G, Y, Z = sizes
    C = 2
    X = Z // C
    NB = Y * Z
    EL, D, HC = gate_weight.shape
    _, HR, WO = down_weight.shape
    TOK, W = tokens.shape
    cw = min(256, HC, WO)
    T, R = NB * TOK, NB * CAP
    NJ, ND = HC // cw, WO // cw
    U = EL * NJ
    NC = 2 * U + EL * ND
    deep = max(D, HR)
    NS = min(NC, (46 << 20) // (deep * cw * 2)) // 2 * 2
    info = jnp.concatenate(
        [expert_ids.astype(F32), gate_probs, jnp.zeros((TOK, 124), F32)], axis=1
    )
    dims = (G, Y, X, C, EL, TOK, W, D, HC, HR, WO, cw, NS)
    dma = pltpu.SemaphoreType.DMA
    vmem = pl.BlockSpec(memory_space=pltpu.VMEM)
    hbm = pl.BlockSpec(memory_space=pl.ANY)
    return pl.pallas_call(
        functools.partial(kernel, dims),
        out_shape=jax.ShapeDtypeStruct((TOK, WO), BF16),
        in_specs=[vmem, vmem, hbm, hbm, hbm],
        out_specs=vmem,
        scratch_shapes=[
            pltpu.VMEM((NS, deep, cw), BF16),
            pltpu.VMEM((G, Y, X, C, TOK, W), BF16),
            pltpu.VMEM((NB, TOK, 128), F32),
            pltpu.VMEM((EL * R, D), BF16),
            pltpu.VMEM((EL * R, T), BF16),
            pltpu.VMEM((T, EL * R), BF16),
            pltpu.VMEM((EL * R, 1), F32),
            pltpu.VMEM((U, G, R, cw), BF16),
            pltpu.VMEM((ND, EL * R, cw), BF16),
            pltpu.VMEM((ND, EL * R, cw), BF16),
            pltpu.VMEM((ND, NB, TOK, cw), BF16),
            pltpu.VMEM((ND, NB, TOK, cw), BF16),
            dma((NS,)),
            dma((NB,)), dma((NB,)),
            dma((G,)), dma((G,)),
            dma((Y,)), dma((Y,)),
            dma((X,)), dma((X,)),
            dma((X,)), dma((X,)),
            dma((Y,)), dma((Y,)),
            dma((2, 2)),
            dma((U, G)), dma((U, G)), dma((U, G)),
            dma((ND, NB)), dma((ND, NB)),
        ],
        compiler_params=pltpu.CompilerParams(
            collective_id=0, has_side_effects=True, vmem_limit_bytes=60 << 20
        ),
        cost_estimate=pl.CostEstimate(
            flops=2 * EL * R * (2 * D * HC + HR * WO),
            bytes_accessed=2 * EL * (2 * D * HC + HR * WO),
            transcendentals=EL * R * HC,
        ),
    )(tokens, info, gate_weight, up_weight, down_weight)


def solution(mesh):
    sizes = (mesh.shape["gx"], mesh.shape["gy"], mesh.shape["gz"])
    return jax.shard_map(
        functools.partial(body, sizes),
        mesh=mesh,
        in_specs=(
            P(("gy", "gz"), "gx"),
            P(("gy", "gz"), None),
            P(("gy", "gz"), None),
            P("gy", None, ("gz", "gx")),
            P("gy", None, ("gz", "gx")),
            P("gy", "gz", "gx"),
        ),
        out_specs=P(("gy", "gz"), "gx"),
        check_vma=False,
    )
```
